128 devices in a mesh: row: 16 (over y_hi, x, core), ad: 8 (over z, y_lo).
Axes of the slice: x: 4, y: 4 (y_hi: 2, y_lo: 2; y = y_hi * 2 + y_lo), z: 4, core: 2. Of those that a mesh axis runs over, the one named last changes fastest.
Arguments:
- tokens: bfloat16 [2048, 8192], P('ad', 'row'), may hold values from -6 to 6
- token_adapter: int32 [2048], P('ad'), may hold values from 0 to 31, as said below
- base_weight: bfloat16 [8192, 16384], P(None, 'row'), may hold values from -1.5 to 1.5
- panel_down: bfloat16 [32, 8192, 64], P(None, ('row', 'ad')), may hold values from -0.5 to 0.5
- panel_up: bfloat16 [32, 64, 16384], P('ad', None, 'row'), may hold values from -0.8984375 to 0.8984375
- magnitude: float32 [32, 16384], P('ad', 'row'), may hold values from 0.5 to 2
Outputs:
- adapted: bfloat16 [2048, 16384], P('ad', 'row')
The draws below stay inside these ranges and needn't reach their ends.
Inputs may be any that keep to these rules, and one draw needn't show every extreme that they name: `token_adapter`: the tokens of the g-th block of 256 tokens name adapters g * 4 to (g + 1) * 4 - 1, never falling within a block.
All inputs are finite; a program needn't handle non-finite values.
Results may differ from the reference program's by a relative error of at most 0.0028.
Values may be sent and summed in bfloat16 or wider, within the bound.
No kernel may reach another device: no remote copies, remote signals or barrier semaphores. Data moves between devices by JAX's collectives and lax.ppermute only.
A program may use at most 128 MiB of HBM per device.

```python
import math
import jax
import jax.numpy as jnp
from jax import lax

D = 8192
FF = 16384
R = 64
NA_DEV = 4
TOK_DEV = 256
NA = 32
TOKENS = 2048


def draw_token_adapter(key, part):
    key = jax.random.fold_in(key, 11)
    group_count = TOKENS // TOK_DEV
    raw_ids = jax.random.randint(key, (group_count, TOK_DEV), 0, NA_DEV)
    ordered = jnp.sort(raw_ids, axis=1)
    offsets = (jnp.arange(group_count, dtype=jnp.int32) * NA_DEV)[:, None]
    return (ordered + offsets).reshape(TOKENS).astype(jnp.int32)


def common_basis(key):
    return jax.random.randint(key, (D, 128), -3, 4).astype(jnp.float32)


def mixed_structure(basis, load_table):
    basis_width = basis.shape[1]
    joined = jnp.dot(basis, load_table, precision=lax.Precision.HIGHEST)
    return joined * (1.0 / (4.0 * math.sqrt(basis_width)))


def scaled_weight(key, noise, row_spread):
    key_rows, key_cols = jax.random.split(key, 2)
    row_scale = jnp.exp(jax.random.uniform(key_rows, (D, 1), jnp.float32, 0.0, math.log(row_spread)))
    col_scale = jnp.exp(jax.random.uniform(key_cols, (1, FF), jnp.float32, 0.0, math.log(10.0)))
    mean_square = (row_spread * row_spread - 1.0) / (2.0 * math.log(row_spread))
    scaled = noise * row_scale * col_scale / math.sqrt(D * mean_square)
    return jnp.clip(scaled, -1.5, 1.5).astype(jnp.bfloat16)


def draw_base_weight(key, part):
    common = common_basis(key)
    key = jax.random.fold_in(key, 23)
    key_noise, key_scale, key_load = jax.random.split(key, 3)
    load_table = jax.random.randint(key_load, (common.shape[1], FF), -3, 4).astype(jnp.float32)
    structure = mixed_structure(common, load_table)
    noise = jnp.clip(jax.random.normal(key_noise, (D, FF), jnp.float32), -6.0, 6.0)
    mixed = jnp.clip(noise + 2.0 * structure, -8.0, 8.0) / math.sqrt(1.0 + 2.0 * 2.0)
    return scaled_weight(key_scale, mixed, 10.0)


def draw_panel_down(key, part):
    common = common_basis(key)
    key = jax.random.fold_in(key, 37)
    key_noise, key_load = jax.random.split(key, 2)
    load_table = jax.random.randint(key_load, (common.shape[1], NA * R), -3, 4).astype(jnp.float32)
    structure = jnp.transpose(mixed_structure(common, load_table).reshape(D, NA, R), (1, 0, 2))
    noise = jnp.clip(jax.random.normal(key_noise, (NA, D, R), jnp.float32), -6.0, 6.0)
    strength = 2.0
    mixed = jnp.clip((noise + strength * structure) / math.sqrt(1.0 + strength * strength), -5.5, 5.5)
    return (mixed / math.sqrt(D)).astype(jnp.bfloat16)


def steps_of(key, extent, shards, smallest, top_value):
    loudness, own = 1.0, jax.random.fold_in(key, 6)
    for position, parts in shards:
        draws = jnp.exp(jax.random.uniform(jax.random.fold_in(own, position), (parts,), jnp.float32, smallest / len(shards), top_value / len(shards)))
        loudness = loudness * jnp.repeat(draws, extent[position] // parts).reshape([-1 if axis == position else 1 for axis in range(len(extent))])
    return loudness


def centred(key, extent, scale, most, shards=(), kind=jnp.bfloat16):
    result = jax.random.normal(key, extent, jnp.float32) * scale
    if len(shards) > 0:
        result = steps_of(key, extent, shards, -0.22, 0.18) * result
    return jnp.clip(result, min=-most, max=most).astype(kind)


def setup_inputs(seed: int = 0) -> dict:
    seeds = jax.random.split(jax.random.key(seed), 7)
    tokens = centred(seeds[0], (TOKENS, D), 1.0, 6.0, ((0, 8), (1, 16)))
    token_adapter = draw_token_adapter(jax.random.fold_in(seeds[6], 71), 0)
    base_weight = draw_base_weight(jax.random.fold_in(seeds[6], 71), 0)
    panel_down = draw_panel_down(jax.random.fold_in(seeds[6], 71), 0)
    panel_up = centred(seeds[4], (NA, R, FF), 0.15, 0.8984375, ((0, 8), (2, 16)))
    magnitude = jnp.clip(jnp.exp(math.log(2.0) - 1.3862944 * jax.random.uniform(seeds[5], (NA, FF), jnp.float32) ** steps_of(seeds[5], (NA, FF), ((0, 8), (1, 16)), -0.2, 0.2)), 0.5, 2.0)
    return dict(tokens=tokens, token_adapter=token_adapter, base_weight=base_weight, panel_down=panel_down, panel_up=panel_up, magnitude=magnitude)


def reference(tokens, token_adapter, base_weight, panel_down, panel_up, magnitude):
    base_term = jnp.dot(tokens, base_weight, preferred_element_type=jnp.float32)
    flat_down = jnp.transpose(panel_down, (1, 0, 2)).reshape(D, NA * R)
    spread = jnp.dot(tokens, flat_down, preferred_element_type=jnp.float32).reshape(TOKENS, NA, R)
    pick_table = (token_adapter[:, None] == jnp.arange(NA, dtype=jnp.int32)[None, :]).astype(jnp.float32)
    low_sum = jnp.einsum('ta,tar->tr', pick_table, spread, precision=lax.Precision.HIGHEST)
    low_round = low_sum.astype(jnp.bfloat16)
    spread_low = (pick_table.astype(jnp.bfloat16)[:, :, None] * low_round[:, None, :]).reshape(TOKENS, NA * R)
    delta_term = jnp.dot(spread_low, panel_up.reshape(NA * R, FF), preferred_element_type=jnp.float32)
    weight_sq = lax.optimization_barrier(jnp.sum(jnp.square(base_weight.astype(jnp.float32)), axis=0))

    def one_norm(index):
        down_panel = panel_down[index]
        up_panel = panel_up[index].astype(jnp.float32)
        cross_term = jnp.dot(down_panel.T, base_weight, preferred_element_type=jnp.float32)
        gram_matrix = jnp.dot(down_panel.T, down_panel, preferred_element_type=jnp.float32)
        gram_bent = jnp.dot(gram_matrix, up_panel, precision=lax.Precision.HIGHEST)
        return weight_sq + 2.0 * lax.optimization_barrier(jnp.sum(cross_term * up_panel, axis=0)) + lax.optimization_barrier(jnp.sum(up_panel * gram_bent, axis=0))
    squares = lax.map(one_norm, jnp.arange(NA, dtype=jnp.int32))
    scale_table = magnitude.astype(jnp.float32) / jnp.sqrt(squares + 1e-06)
    tok_scale = jnp.dot(pick_table, scale_table, precision=lax.Precision.HIGHEST)
    return (tok_scale * (base_term + delta_term)).astype(jnp.bfloat16)
```

```python
import jax
import jax.numpy as jnp
from jax import lax
from jax.experimental import pallas as pl
from jax.experimental.pallas import tpu as pltpu
from jax.sharding import PartitionSpec as P

F32, BF16 = jnp.float32, jnp.bfloat16
VM = pl.BlockSpec(memory_space=pltpu.VMEM)
SM = pl.BlockSpec(memory_space=pltpu.SMEM)
NT = (((1,), (1,)), ((), ()))
TN = 256
MIB = 1 << 20

ROWS = [(yh, x, c) for yh in range(2) for x in range(4) for c in range(2)]
ADS = [(z, yl) for z in range(4) for yl in range(2)]


def row_of(yh, x, c):
    return (yh * 4 + x) * 2 + c


RING = [(row_of(yh, x, c), row_of(yh, (x + 1 - 2 * c) % 4, c)) for yh, x, c in ROWS]
CORE = [(row_of(yh, x, c), row_of(yh, x, 1 - c)) for yh, x, c in ROWS]
PAIR = [(row_of(yh, x, c), row_of(1 - yh, x, c)) for yh, x, c in ROWS]
YLO = [(z * 2 + yl, z * 2 + 1 - yl) for z, yl in ADS]


def ring(a):
    return lax.ppermute(a, "row", RING)


def core(a):
    return lax.ppermute(a, "row", CORE)


def pair(a):
    return lax.ppermute(a, "row", PAIR)


def ylo(a):
    return lax.ppermute(a, "ad", YLO)


def zshift(a, step):
    return lax.ppermute(a, "ad", [(z * 2 + yl, (z + step) % 4 * 2 + yl) for z, yl in ADS])


def tie(a, *after):
    return lax.optimization_barrier((a,) + after)[0]


def cat(*parts):
    return jnp.concatenate(parts, 0)


def params(limit=8 * MIB):
    return pltpu.CompilerParams(vmem_limit_bytes=limit)


def pack_body(pos_ref, d_ref, mine_ref, send_ref):
    z, yl = pos_ref[0], pos_ref[1]
    for out_ref, lane in ((mine_ref, yl), (send_ref, 1 - yl)):
        for j in range(4):
            group = lax.rem(z + j, 4) * 2 + lane
            four = d_ref[pl.ds(group * 4, 4)]
            out_ref[j] = jnp.concatenate([four[a] for a in range(4)], axis=1)


def pack(pos, panel):
    d, r = panel.shape[1:]
    shape = jax.ShapeDtypeStruct((4, d, 4 * r), BF16)
    return pl.pallas_call(
        pack_body,
        out_shape=[shape, shape],
        in_specs=[SM, VM],
        out_specs=[VM, VM],
        name="pack",
        cost_estimate=pl.CostEstimate(flops=0, bytes_accessed=MIB, transcendentals=0),
        compiler_params=params(),
    )(pos, panel)


def join_body(pos_ref, a0, a1, a2, a3, out_ref, full):
    z, yl = pos_ref[0], pos_ref[1]
    d = a0.shape[1]
    for ref, back in ((a0, 0), (a1, 3), (a2, 2), (a3, 1)):
        src = lax.rem(z + back, 4) * 2
        full[pl.ds(pl.multiple_of((src + yl) * d, d), d), :] = ref[0]
        full[pl.ds(pl.multiple_of((src + 1 - yl) * d, d), d), :] = ref[1]
    out_ref[...] = full[...].T


def join(pos, *pieces):
    _, d, width = pieces[0].shape
    return pl.pallas_call(
        join_body,
        out_shape=jax.ShapeDtypeStruct((width, 8 * d), BF16),
        in_specs=[SM] + [VM] * 4,
        out_specs=VM,
        scratch_shapes=[pltpu.VMEM((8 * d, width), BF16)],
        name="join",
        cost_estimate=pl.CostEstimate(flops=0, bytes_accessed=MIB, transcendentals=0),
        compiler_params=params(),
    )(pos, *pieces)


def halves(refs, height):
    return [(ref, h) for ref in refs for h in range(ref.shape[0] // height)]


def rows_at(block, height):
    ref, h = block
    return ref[h * height : (h + 1) * height, :]


def token_step(name, ids, blocks, weight, state):
    count = len(blocks)
    height, depth = blocks[0].shape[0], blocks[0].shape[1]
    height = 256 if height > 256 else height
    cols = weight.shape[1]
    first = state is None

    def body(ids_ref, *refs):
        held = halves(refs[:count], height)
        w_ref = refs[count]
        base_in, sq_in = (None, None) if first else refs[count + 1 : count + 3]
        base_out, sq_out = refs[-2:]
        for lo in range(0, cols, TN):
            tile = slice(lo, lo + TN)
            total = None if first else base_in[:, tile]
            squares = None if first else sq_in[:, tile]
            for i, block in enumerate(held):
                start = pl.multiple_of(ids_ref[i] * depth, depth)
                w = w_ref[pl.ds(start, depth), tile]
                part = jnp.dot(rows_at(block, height), w, preferred_element_type=F32)
                total = part if total is None else total + part
                wide = w.astype(F32)
                sq = jnp.sum((wide * wide).reshape(depth // 8, 8, TN), axis=0)
                squares = sq if squares is None else squares + sq
            base_out[:, tile] = total
            sq_out[:, tile] = squares

    n = sum(b.shape[0] // height for b in blocks)
    return pl.pallas_call(
        body,
        out_shape=[
            jax.ShapeDtypeStruct((height, cols), F32),
            jax.ShapeDtypeStruct((8, cols), F32),
        ],
        in_specs=[SM] + [VM] * (count + 1 + (0 if first else 2)),
        out_specs=[VM, VM],
        input_output_aliases={} if first else {count + 2: 0, count + 3: 1},
        name=name,
        cost_estimate=pl.CostEstimate(
            flops=2 * n * height * depth * cols, bytes_accessed=n * MIB, transcendentals=0
        ),
        compiler_params=params(),
    )(ids, *blocks, weight, *([] if first else state))


def panel_step(name, ids, tokens, panels, weight, state):
    count = len(panels)
    depth = panels[0].shape[1]
    height = 256
    cols = weight.shape[1]
    first = state is None

    def body(ids_ref, *refs):
        tok = halves(refs[:count], height)
        pan = halves(refs[count : 2 * count], height)
        w_ref = refs[2 * count]
        cross_in, both_in = (None, None) if first else refs[2 * count + 1 : 2 * count + 3]
        cross_out, both_out = refs[-2:]
        for lo in range(0, cols, TN):
            tile = slice(lo, lo + TN)
            total = None if first else cross_in[:, tile]
            for i, block in enumerate(pan):
                start = pl.multiple_of(ids_ref[i] * depth, depth)
                w = w_ref[pl.ds(start, depth), tile]
                part = jnp.dot(rows_at(block, height), w, preferred_element_type=F32)
                total = part if total is None else total + part
            cross_out[:, tile] = total
        for j, left in enumerate((tok, pan)):
            band = slice(j * height, (j + 1) * height)
            total = None if first else both_in[band, :]
            for a, b in zip(left, pan):
                part = lax.dot_general(
                    rows_at(a, height), rows_at(b, height), NT, preferred_element_type=F32
                )
                total = part if total is None else total + part
            both_out[band, :] = total

    n = sum(b.shape[0] // height for b in panels)
    return pl.pallas_call(
        body,
        out_shape=[
            jax.ShapeDtypeStruct((height, cols), F32),
            jax.ShapeDtypeStruct((2 * height, height), F32),
        ],
        in_specs=[SM] + [VM] * (2 * count + 1 + (0 if first else 2)),
        out_specs=[VM, VM],
        input_output_aliases={} if first else {2 * count + 2: 0, 2 * count + 3: 1},
        name=name,
        cost_estimate=pl.CostEstimate(
            flops=2 * n * height * depth * (cols + 2 * height),
            bytes_accessed=n * MIB,
            transcendentals=0,
        ),
        compiler_params=params(),
    )(ids, *tokens, *panels, weight, *([] if first else state))


def finish_body(base_ref, sq_ref, cross_ref, both_ref, up_ref, mag_ref, id_ref, out_ref):
    adapters = mag_ref.shape[0]
    tokens, cols = base_ref.shape
    width = cross_ref.shape[0]
    rank = width // adapters
    own = id_ref[...]
    lane = lax.broadcasted_iota(jnp.int32, (tokens, width), 1) // rank
    own_wide = jnp.concatenate([own] * (width // 128), axis=1)
    low = jnp.where(lane == own_wide, both_ref[:tokens, :], 0.0).astype(BF16)
    line = lax.broadcasted_iota(jnp.int32, (width, width), 0) // rank
    side = lax.broadcasted_iota(jnp.int32, (width, width), 1) // rank
    gram = jnp.where(line == side, both_ref[tokens:, :], 0.0)
    gram_hi = gram.astype(BF16)
    gram_lo = (gram - gram_hi.astype(F32)).astype(BF16)
    left = jnp.concatenate([low, gram_hi, gram_lo], axis=0)
    own_tile = jnp.concatenate([own] * (TN // 128), axis=1)
    for lo in range(0, cols, TN):
        tile = slice(lo, lo + TN)
        up = up_ref[:, tile]
        prod = jnp.dot(left, up, preferred_element_type=F32)
        delta = prod[:tokens]
        bent = prod[tokens : tokens + width] + prod[tokens + width :]
        terms = up.astype(F32) * (2.0 * cross_ref[:, tile] + bent)
        weight_sq = jnp.sum(sq_ref[:, tile], axis=0, keepdims=True)
        scale = None
        for a in range(adapters):
            mine = jnp.sum(terms[a * rank : (a + 1) * rank], axis=0, keepdims=True)
            gain = mag_ref[a : a + 1, tile] / jnp.sqrt(weight_sq + mine + 1e-6)
            wide = jnp.broadcast_to(gain, (tokens, TN))
            scale = wide if scale is None else jnp.where(own_tile == a, wide, scale)
        out_ref[:, tile] = (scale * (base_ref[:, tile] + delta)).astype(BF16)


def finish(base, sq, cross, both, up, mag, ids):
    tokens, cols = base.shape
    return pl.pallas_call(
        finish_body,
        out_shape=jax.ShapeDtypeStruct((tokens, cols), BF16),
        in_specs=[VM] * 7,
        out_specs=VM,
        name="finish",
        compiler_params=params(16 * MIB),
    )(base, sq, cross, both, up, mag, ids)


def on_device(tokens, token_adapter, base_weight, panel_down, panel_up, magnitude):
    adapters, rank, cols = panel_up.shape
    row = lax.axis_index("row").astype(jnp.int32)
    ad = lax.axis_index("ad").astype(jnp.int32)
    c, x, yh = row % 2, row // 2 % 4, row // 8
    step = 1 - 2 * c

    def at(dy, dx, dc):
        return (((yh + dy) % 2) * 4 + (x + dx * step + 8) % 4) * 2 + (c + dc) % 2

    def ids(*places):
        return jnp.stack([at(*p) for p in places])

    own, behind, ahead, far = (0, 0), (0, -1), (0, 1), (0, 2)
    p_own, p_behind, p_ahead, p_far = (1, 0), (1, -1), (1, 1), (1, 2)
    straight = lambda p: ((*p, 0), (*p, 1))
    crossed = lambda p: ((*p, 1), (*p, 0))

    pos = jnp.stack([ad // 2, ad % 2])
    up = panel_up.reshape(adapters * rank, cols)
    local = jnp.broadcast_to((token_adapter - ad * adapters)[:, None], (tokens.shape[0], 128))

    t0 = tokens
    o1 = core(t0)
    mine, send = pack(pos, panel_down)
    got = ylo(send)
    t_pair = pair(t0)
    t_ring = ring(cat(t0, o1))
    got = tie(got, o1)
    z_own = jnp.stack([mine[0], got[0]])
    z1 = zshift(jnp.stack([mine[1], got[1]]), 1)
    z3 = zshift(jnp.stack([mine[3], got[3]]), 3)
    z2 = zshift(jnp.stack([mine[2], got[2]]), 2)
    t_pair_c = core(t_pair)
    t_far = ring(t_ring[:256])
    t_pair_ring = ring(cat(t_pair, t_pair_c))
    z_own, z1, z2, z3 = tie((z_own, z1, z2, z3), t_ring, t_pair)
    q = join(pos, z_own, z1, z2, z3)
    base = token_step("tok_a", ids(*straight(own)), [t0, o1], base_weight, None)
    t_ring_c = core(t_ring)

    d_pair = pair(q)
    po = core(q)
    d_ring_a = ring(tie(q, t_far))
    d_ring_b = ring(po)
    base = token_step("tok_b", ids(*straight(behind), *crossed(ahead)), [t_ring, t_ring_c], base_weight, base)
    t_far_c = core(t_far)
    t_far_pair = pair(t_far)
    t_pair_ring_c = core(t_pair_ring)
    base = token_step(
        "tok_c",
        ids(*straight(p_own), *straight(far)),
        [t_pair, t_pair_c, t_far, t_far_c],
        base_weight,
        base,
    )
    norm = panel_step("pan_a", ids(*straight(own)), [t0, o1], [q, po], base_weight, None)
    d_pair_c = core(d_pair)
    d_far = ring(d_ring_a)
    d_pair_ring = ring(tie(cat(d_pair, d_pair_c), d_ring_b))
    t_far_pair_c = core(t_far_pair)
    base = token_step(
        "tok_d",
        ids(*straight(p_behind), *crossed(p_ahead), *straight(p_far)),
        [t_pair_ring, t_pair_ring_c, t_far_pair, t_far_pair_c],
        base_weight,
        base,
    )
    d_ring_ac, d_ring_bc = core(d_ring_a), core(d_ring_b)
    norm = panel_step(
        "pan_b",
        ids(*straight(behind), (*ahead, 1), (*ahead, 0), *straight(p_own)),
        [t_ring[:256], t_ring[256:], t_ring_c[:256], t_ring_c[256:], t_pair, t_pair_c],
        [d_ring_a, d_ring_b, d_ring_ac, d_ring_bc, d_pair, d_pair_c],
        base_weight,
        norm,
    )
    d_far_c = core(d_far)
    d_far_pair = pair(d_far)
    norm = panel_step("pan_c", ids(*straight(far)), [t_far, t_far_c], [d_far, d_far_c], base_weight, norm)
    d_pair_ring_c = core(d_pair_ring)
    norm = panel_step(
        "pan_d",
        ids(*straight(p_behind), *crossed(p_ahead)),
        [t_pair_ring, t_pair_ring_c],
        [d_pair_ring, d_pair_ring_c],
        base_weight,
        norm,
    )
    d_far_pair_c = core(d_far_pair)
    norm = panel_step(
        "pan_e", ids(*straight(p_far)), [t_far_pair, t_far_pair_c], [d_far_pair, d_far_pair_c], base_weight, norm
    )
    return finish(*base, *norm, up, magnitude, local)


def solution(mesh):
    placed = (
        P("ad", "row"),
        P("ad"),
        P(None, "row"),
        P(None, ("row", "ad"), None),
        P("ad", None, "row"),
        P("ad", "row"),
    )
    return jax.shard_map(on_device, mesh=mesh, in_specs=placed, out_specs=P("ad", "row"), check_vma=False)
```

```python
import jax
import jax.numpy as jnp
from jax import lax
from jax.experimental import pallas as pl
from jax.experimental.pallas import tpu as pltpu
from jax.sharding import PartitionSpec as P

F32, BF16 = jnp.float32, jnp.bfloat16
ANY = pl.BlockSpec(memory_space=pltpu.HBM)
VM = pl.BlockSpec(memory_space=pltpu.VMEM)
SM = pl.BlockSpec(memory_space=pltpu.SMEM)
NT = (((1,), (1,)), ((), ()))
TN = 512
MIB = 1 << 20

ROWS = [(yh, x, c) for yh in range(2) for x in range(4) for c in range(2)]
ADS = [(z, yl) for z in range(4) for yl in range(2)]


def row_of(yh, x, c):
    return (yh * 4 + x) * 2 + c


RING = [(row_of(yh, x, c), row_of(yh, (x + 1 - 2 * c) % 4, c)) for yh, x, c in ROWS]
CORE = [(row_of(yh, x, c), row_of(yh, x, 1 - c)) for yh, x, c in ROWS]
PAIR = [(row_of(yh, x, c), row_of(1 - yh, x, c)) for yh, x, c in ROWS]
YLO = [(z * 2 + yl, z * 2 + 1 - yl) for z, yl in ADS]


def ring(a):
    return lax.ppermute(a, "row", RING)


def core(a):
    return lax.ppermute(a, "row", CORE)


def pair(a):
    return lax.ppermute(a, "row", PAIR)


def ylo(a):
    return lax.ppermute(a, "ad", YLO)


def zshift(a, step):
    return lax.ppermute(a, "ad", [(z * 2 + yl, (z + step) % 4 * 2 + yl) for z, yl in ADS])


class Line:
    def __init__(self):
        self.done = ()

    def after(self, a):
        return lax.optimization_barrier((a, *self.done))[0] if self.done else a

    def send(self, how, a):
        return how(self.after(a))

    def got(self, *values):
        self.done += values

    def ran(self, value):
        self.done = (value,)


def cat(*parts):
    return jnp.concatenate(parts, 0)


def cost():
    return pl.CostEstimate(flops=1024, bytes_accessed=1024, transcendentals=0)


def call(body, name, inputs, specs, outs, scratch=(), aliases=None, limit=8 * MIB, out_specs=None):
    return pl.pallas_call(
        body,
        out_shape=outs,
        in_specs=specs,
        out_specs=out_specs or [VM] * len(outs),
        scratch_shapes=list(scratch),
        input_output_aliases=aliases or {},
        name=name,
        cost_estimate=cost(),
        compiler_params=pltpu.CompilerParams(vmem_limit_bytes=limit),
    )(*inputs)


def pack_body(pos_ref, d_ref, mine_ref, send_ref):
    z, yl = pos_ref[0], pos_ref[1]
    for out_ref, lane in ((mine_ref, yl), (send_ref, 1 - yl)):
        for j in range(4):
            group = lax.rem(z + j, 4) * 2 + lane
            four = d_ref[pl.ds(group * 4, 4)]
            out_ref[j] = jnp.concatenate([four[a] for a in range(4)], axis=1)


def pack(pos, panel):
    d, r = panel.shape[1:]
    shape = jax.ShapeDtypeStruct((4, d, 4 * r), BF16)
    return call(pack_body, "pack", (pos, panel), [SM, VM], [shape, shape])


def join_body(pos_ref, a0, a1, a2, a3, out_ref, full):
    z, yl = pos_ref[0], pos_ref[1]
    d = a0.shape[1]
    for ref, back in ((a0, 0), (a1, 3), (a2, 2), (a3, 1)):
        src = lax.rem(z + back, 4) * 2
        full[pl.ds(pl.multiple_of((src + yl) * d, d), d), :] = ref[0]
        full[pl.ds(pl.multiple_of((src + 1 - yl) * d, d), d), :] = ref[1]
    out_ref[...] = full[...].T


def join(pos, *pieces):
    _, d, width = pieces[0].shape
    outs = [jax.ShapeDtypeStruct((width, 8 * d), BF16)]
    scratch = [pltpu.VMEM((8 * d, width), BF16)]
    return call(join_body, "join", (pos, *pieces), [SM] + [VM] * 4, outs, scratch)[0]


OWN = ((0, 0, 0), (0, 0, 1))
BEHIND = ((0, -1, 0), (0, -1, 1))
AHEAD = ((0, 1, 1), (0, 1, 0))
FAR = ((0, 2, 0), (0, 2, 1))


def mirrored(places):
    return tuple((1 - dy, dx, dc) for dy, dx, dc in places)


def weight_row(pos_ref, place, depth):
    dy, dx, dc = place
    c, x, yh = pos_ref[2], pos_ref[3], pos_ref[4]
    side = lax.rem(x + dx * (1 - 2 * c) + 4, 4)
    block = (lax.rem(yh + dy, 2) * 4 + side) * 2 + lax.rem(c + dc, 2)
    return pl.multiple_of(block * depth, depth)


def view(ref, h):
    return ref[h * 256 : (h + 1) * 256, :]


class Operands:
    def __init__(self):
        self.arrays = []

    def add(self, block):
        array, h = block if isinstance(block, tuple) else (block, 0)
        for i, known in enumerate(self.arrays):
            if known is array:
                return i, h
        self.arrays.append(array)
        return len(self.arrays) - 1, h


def squared(w):
    wide = w.astype(F32)
    return jnp.sum((wide * wide).reshape(w.shape[0] // 8, 8, w.shape[1]), axis=0)


def plus(a, b):
    return b if a is None else a + b


def tiles(cols):
    return [slice(lo, lo + TN) for lo in range(0, cols, TN)]


def nt(a, b):
    return lax.dot_general(a, b, NT, preferred_element_type=F32)


def spread_and_gram(refs, pans, spread, gram):
    for _, (i, g), (k, h) in pans:
        d = view(refs[k], h)
        spread = plus(spread, nt(view(refs[i], g), d))
        gram = plus(gram, nt(d, d))
    return spread, gram


def accumulators(cols, with_base, with_norm):
    shapes = [(256, cols), (8, cols)] * with_base + [(256, cols), (512, 256)] * with_norm
    return [jax.ShapeDtypeStruct(shape, F32) for shape in shapes]


def first_step(pos, both, toks, weight):
    ops = Operands()
    both = [(p, ops.add(t), ops.add(d)) for p, t, d in both]
    toks = [(p, ops.add(t)) for p, t in toks]
    count = len(ops.arrays)
    rows, cols = weight.shape
    depth = ops.arrays[0].shape[1]
    order = [item[0] for item in both + toks]
    order += [p for p in OWN + BEHIND + AHEAD + FAR if p not in order]
    order += mirrored(OWN + BEHIND + AHEAD + FAR)

    def body(pos_ref, *refs):
        hbm = refs[count]
        w_ref, base_out, sq_out, cross_out, both_out, sems = refs[count + 1 :]
        starts, copies = [], []
        for i, p in enumerate(order):
            starts.append(weight_row(pos_ref, p, depth))
            at = pl.ds(starts[i], depth)
            copies.append(pltpu.make_async_copy(hbm.at[at, :], w_ref.at[at, :], sems.at[i]))
            copies[i].start()
        spread, gram = spread_and_gram(refs, both, None, None)
        both_out[:256, :], both_out[256:, :] = spread, gram
        for i, item in enumerate(both + toks):
            copies[i].wait()
            for tile in tiles(cols):
                w = w_ref[pl.ds(starts[i], depth), tile]
                left = jnp.concatenate([view(refs[a], h) for a, h in item[1:]], axis=0)
                part = jnp.dot(left, w, preferred_element_type=F32)
                base, sq = part[:256], squared(w)
                base_out[:, tile] = base if i == 0 else base_out[:, tile] + base
                sq_out[:, tile] = sq if i == 0 else sq_out[:, tile] + sq
                if i < len(both):
                    cross = part[256:]
                    cross_out[:, tile] = cross if i == 0 else cross_out[:, tile] + cross
        for i in range(len(both + toks), len(order)):
            copies[i].wait()

    return call(
        body,
        "first",
        (pos, *ops.arrays, weight),
        [SM] + [VM] * count + [ANY],
        [jax.ShapeDtypeStruct((rows, cols), BF16)] + accumulators(cols, True, True),
        [pltpu.SemaphoreType.DMA((len(order),))],
        limit=30 * MIB,
    )


def step(name, pos, toks, pans, weight, base, norm):
    ops = Operands()
    toks = [(p, ops.add(t)) for p, t in toks]
    pans = [(p, ops.add(t), ops.add(d)) for p, t, d in pans]
    count = len(ops.arrays)
    depth, cols = ops.arrays[0].shape[1], weight.shape[1]
    state = (list(base) if toks else []) + (list(norm) if pans else [])
    n = len(state)

    def body(pos_ref, *refs):
        w_ref = refs[count]
        ins, outs = refs[count + 1 : count + 1 + n], refs[count + 1 + n :]
        if pans:
            spread, gram = spread_and_gram(refs, pans, ins[-1][:256, :], ins[-1][256:, :])
            outs[-1][:256, :], outs[-1][256:, :] = spread, gram
        tok_rows = [weight_row(pos_ref, item[0], depth) for item in toks]
        pan_rows = [weight_row(pos_ref, item[0], depth) for item in pans]
        for tile in tiles(cols):
            if toks:
                total, sq = ins[0][:, tile], ins[1][:, tile]
                for row, (_, (a, h)) in zip(tok_rows, toks):
                    w = w_ref[pl.ds(row, depth), tile]
                    total = total + jnp.dot(view(refs[a], h), w, preferred_element_type=F32)
                    sq = sq + squared(w)
                outs[0][:, tile], outs[1][:, tile] = total, sq
            if pans:
                total = ins[-2][:, tile]
                for row, (_, _, (a, h)) in zip(pan_rows, pans):
                    w = w_ref[pl.ds(row, depth), tile]
                    total = total + jnp.dot(view(refs[a], h), w, preferred_element_type=F32)
                outs[-2][:, tile] = total

    new = call(
        body,
        name,
        (pos, *ops.arrays, weight, *state),
        [SM] + [VM] * (count + 1 + n),
        accumulators(cols, bool(toks), bool(pans)),
        aliases={count + 2 + i: i for i in range(n)},
    )
    return (new[:2] if toks else base), (new[-2:] if pans else norm)


def last_step(pos, both, pans, weight, base, norm, up, mag, ids):
    ops = Operands()
    both, pans = ([(p, ops.add(t), ops.add(d)) for p, t, d in work] for work in (both, pans))
    count = len(ops.arrays)
    depth, cols = ops.arrays[0].shape[1], weight.shape[1]
    adapters, width, tokens = mag.shape[0], up.shape[0], base[0].shape[0]
    rank = width // adapters

    def body(pos_ref, *refs):
        w_ref, base_ref, sq_ref, cross_ref, both_ref, up_ref, mag_ref, id_ref = refs[count : count + 8]
        out_ref, held, sems = refs[count + 8 :]
        spread, gram = spread_and_gram(refs, both + pans, both_ref[:tokens, :], both_ref[tokens:, :])
        both_rows = [weight_row(pos_ref, item[0], depth) for item in both]
        rows = [weight_row(pos_ref, item[0], depth) for item in pans]
        local = id_ref[...] - (pos_ref[0] * 2 + pos_ref[1]) * adapters
        own = jnp.broadcast_to(local, (128, tokens)).T
        lane = lax.broadcasted_iota(jnp.int32, (tokens, width), 1) // rank
        own_wide = jnp.concatenate([own] * (width // 128), axis=1)
        low = jnp.where(lane == own_wide, spread, 0.0).astype(BF16)
        line = lax.broadcasted_iota(jnp.int32, (width, width), 0) // rank
        side = lax.broadcasted_iota(jnp.int32, (width, width), 1) // rank
        gram = jnp.where(line == side, gram, 0.0)
        gram_hi = gram.astype(BF16)
        gram_lo = (gram - gram_hi.astype(F32)).astype(BF16)
        left = jnp.concatenate([low, gram_hi, gram_lo], axis=0)
        own_tile = jnp.concatenate([own] * (TN // 128), axis=1)
        copies = []
        for n, tile in enumerate(tiles(cols)):
            base, sq, cross = base_ref[:, tile], sq_ref[:, tile], cross_ref[:, tile]
            for row, item in zip(both_rows, both):
                w = w_ref[pl.ds(row, depth), tile]
                pair_of = jnp.concatenate([view(refs[a], h) for a, h in item[1:]], axis=0)
                part = jnp.dot(pair_of, w, preferred_element_type=F32)
                base, cross, sq = base + part[:tokens], cross + part[tokens:], sq + squared(w)
            for row, (_, _, (a, h)) in zip(rows, pans):
                w = w_ref[pl.ds(row, depth), tile]
                cross = cross + jnp.dot(view(refs[a], h), w, preferred_element_type=F32)
            up_tile = up_ref[:, tile]
            prod = jnp.dot(left, up_tile, preferred_element_type=F32)
            bent = prod[tokens : tokens + width] + prod[tokens + width :]
            terms = up_tile.astype(F32) * (2.0 * cross + bent)
            weight_sq = jnp.sum(sq, axis=0, keepdims=True)
            scale = None
            for a in range(adapters):
                mine = jnp.sum(terms[a * rank : (a + 1) * rank], axis=0, keepdims=True)
                gain = mag_ref[a : a + 1, tile] / jnp.sqrt(weight_sq + mine + 1e-6)
                wide = jnp.broadcast_to(gain, (tokens, TN))
                scale = wide if scale is None else jnp.where(own_tile == a, wide, scale)
            held[n] = (scale * (base + prod[:tokens])).astype(BF16)
            copies.append(pltpu.make_async_copy(held.at[n], out_ref.at[:, tile], sems.at[n]))
            copies[n].start()
        for copy in copies:
            copy.wait()

    inputs = (pos, *ops.arrays, weight, *base, *norm, up, mag, ids)
    outs = [jax.ShapeDtypeStruct((tokens, cols), BF16)]
    scratch = [pltpu.VMEM((cols // TN, tokens, TN), BF16), pltpu.SemaphoreType.DMA((cols // TN,))]
    return call(body, "last", inputs, [SM] + [VM] * (count + 8), outs, scratch, out_specs=[ANY])[0]


def on_device(tokens, token_adapter, base_weight, panel_down, panel_up, magnitude):
    adapters, rank, cols = panel_up.shape
    row = lax.axis_index("row").astype(jnp.int32)
    ad = lax.axis_index("ad").astype(jnp.int32)
    pos = jnp.stack([ad // 2, ad % 2, row % 2, row // 2 % 4, row // 8])
    up = panel_up.reshape(adapters * rank, cols)

    line = Line()
    line.ran(pos)
    tc = line.send(core, tokens)
    tr = line.send(ring, tokens)
    mine, away = pack(line.after(pos), panel_down)
    line.ran(away)
    line.got(tc)

    got = line.send(ylo, away)
    tr2 = line.send(ring, tc)
    tp = line.send(pair, tokens)
    t = line.send(core, tc)
    line.got(got, tr, t)

    z1 = line.send(lambda a: zshift(a, 1), jnp.stack([mine[1], got[1]]))
    z3 = line.send(lambda a: zshift(a, -1), jnp.stack([mine[3], got[3]]))
    z2 = line.send(lambda a: zshift(a, 2), jnp.stack([mine[2], got[2]]))
    line.got(z1, z3, z2, tr2, tp)
    d = join(line.after(pos), jnp.stack([mine[0], got[0]]), z1, z2, z3)
    line.ran(d)

    dr = line.send(ring, d)
    dc = line.send(core, d)
    dp = line.send(pair, d)
    tpc = line.send(core, tp)
    trc = line.send(core, cat(tr, tr2))
    line.got(dc, trc, tpc)
    dr2 = line.send(ring, dc)
    tf = line.send(ring, tr)
    tpr = line.send(ring, cat(tp, tpc))
    w, *sums = first_step(
        line.after(pos),
        list(zip(OWN, [t, tc], [d, dc])),
        list(zip(BEHIND + AHEAD, [tr, tr2, (trc, 0), (trc, 1)])),
        base_weight,
    )
    base, norm = sums[:2], sums[2:]
    line.ran(norm[1])
    line.got(dr, dr2, dp, tf)

    df = line.send(ring, dr)
    tfp = line.send(pair, tf)
    dpc = line.send(core, dp)
    drc = line.send(core, cat(dr, dr2))
    base, norm = step(
        "mid_a",
        line.after(pos),
        list(zip(mirrored(OWN), [tp, tpc])),
        list(zip(BEHIND, [tr, tr2], [dr, dr2])),
        w,
        base,
        norm,
    )
    line.ran(norm[1])
    line.got(df, dpc, drc, tpr, tfp)

    dpr = line.send(ring, cat(dp, dpc))
    dfp = line.send(pair, df)
    tprc = line.send(core, tpr)
    tfc = line.send(core, tf)
    tfpc = line.send(core, tfp)
    base, norm = step(
        "mid_b",
        line.after(pos),
        list(zip(mirrored(BEHIND), [(tpr, 0), (tpr, 1)])),
        list(zip(AHEAD + mirrored(OWN), [(trc, 0), (trc, 1), tp, tpc], [(drc, 0), (drc, 1), dp, dpc])),
        w,
        base,
        norm,
    )
    line.ran(norm[1])
    line.got(tprc, tfc, tfpc, dpr, dfp)

    dprc = line.send(core, dpr)
    dfpc = line.send(core, dfp)
    dfc = line.send(core, df)
    base, norm = step(
        "mid_c", line.after(pos), list(zip(FAR + mirrored(AHEAD), [tf, tfc, (tprc, 0), (tprc, 1)])), [], w, base, norm
    )
    line.ran(base[1])
    line.got(dfpc, dprc, dfc)
    ring_t = [(tpr, 0), (tpr, 1), (tprc, 0), (tprc, 1)]
    ring_d = [(dpr, 0), (dpr, 1), (dprc, 0), (dprc, 1)]
    return last_step(
        line.after(pos),
        list(zip(mirrored(FAR), [tfp, tfpc], [dfp, dfpc])),
        list(zip(FAR + mirrored(BEHIND + AHEAD), [tf, tfc] + ring_t, [df, dfc] + ring_d)),
        w,
        base,
        norm,
        up,
        magnitude,
        token_adapter[None, :],
    )


def solution(mesh):
    placed = (
        P("ad", "row"),
        P("ad"),
        P(None, "row"),
        P(None, ("row", "ad"), None),
        P("ad", None, "row"),
        P("ad", "row"),
    )
    return jax.shard_map(on_device, mesh=mesh, in_specs=placed, out_specs=P("ad", "row"), check_vma=False)
```

```python
import jax
import jax.numpy as jnp
from jax import lax
from jax.experimental import pallas as pl
from jax.experimental.pallas import tpu as pltpu
from jax.sharding import PartitionSpec as P

F32, BF16 = jnp.float32, jnp.bfloat16
ANY = pl.BlockSpec(memory_space=pltpu.HBM)
VM = pl.BlockSpec(memory_space=pltpu.VMEM)
SM = pl.BlockSpec(memory_space=pltpu.SMEM)
NT = (((1,), (1,)), ((), ()))
TN = 512
MIB = 1 << 20

ROWS = [(yh, x, c) for yh in range(2) for x in range(4) for c in range(2)]
ADS = [(z, yl) for z in range(4) for yl in range(2)]


def row_of(yh, x, c):
    return (yh * 4 + x) * 2 + c


RING = [(row_of(yh, x, c), row_of(yh, (x + 1 - 2 * c) % 4, c)) for yh, x, c in ROWS]
CORE = [(row_of(yh, x, c), row_of(yh, x, 1 - c)) for yh, x, c in ROWS]
PAIR = [(row_of(yh, x, c), row_of(1 - yh, x, c)) for yh, x, c in ROWS]
YLO = [(z * 2 + yl, z * 2 + 1 - yl) for z, yl in ADS]


def ring(a):
    return lax.ppermute(a, "row", RING)


def core(a):
    return lax.ppermute(a, "row", CORE)


def pair(a):
    return lax.ppermute(a, "row", PAIR)


def ylo(a):
    return lax.ppermute(a, "ad", YLO)


def zshift(a, step):
    return lax.ppermute(a, "ad", [(z * 2 + yl, (z + step) % 4 * 2 + yl) for z, yl in ADS])


class Line:
    def __init__(self):
        self.done = ()

    def after(self, a):
        return lax.optimization_barrier((a, *self.done))[0] if self.done else a

    def send(self, how, a):
        return how(self.after(a))

    def got(self, *values):
        self.done += values

    def ran(self, value):
        self.done = (value,)


def cat(*parts):
    return jnp.concatenate(parts, 0)


def cost():
    return pl.CostEstimate(flops=1024, bytes_accessed=1024, transcendentals=0)


def call(body, name, inputs, specs, outs, scratch=(), aliases=None, limit=8 * MIB, out_specs=None):
    return pl.pallas_call(
        body,
        out_shape=outs,
        in_specs=specs,
        out_specs=out_specs or [VM] * len(outs),
        scratch_shapes=list(scratch),
        input_output_aliases=aliases or {},
        name=name,
        cost_estimate=cost(),
        compiler_params=pltpu.CompilerParams(vmem_limit_bytes=limit),
    )(*inputs)


def pack_body(pos_ref, d_ref, mine_ref, send_ref):
    z, yl = pos_ref[0], pos_ref[1]
    for out_ref, lane in ((mine_ref, yl), (send_ref, 1 - yl)):
        for j in range(4):
            group = lax.rem(z + j, 4) * 2 + lane
            four = d_ref[pl.ds(group * 4, 4)]
            out_ref[j] = jnp.concatenate([four[a] for a in range(4)], axis=1)


def pack(pos, panel):
    d, r = panel.shape[1:]
    shape = jax.ShapeDtypeStruct((4, d, 4 * r), BF16)
    return call(pack_body, "pack", (pos, panel), [SM, VM], [shape, shape])


def join_body(pos_ref, a0, a1, a2, a3, out_ref, full):
    z, yl = pos_ref[0], pos_ref[1]
    d = a0.shape[1]
    for ref, back in ((a0, 0), (a1, 3), (a2, 2), (a3, 1)):
        src = lax.rem(z + back, 4) * 2
        full[pl.ds(pl.multiple_of((src + yl) * d, d), d), :] = ref[0]
        full[pl.ds(pl.multiple_of((src + 1 - yl) * d, d), d), :] = ref[1]
    out_ref[...] = full[...].T


def join(pos, *pieces):
    _, d, width = pieces[0].shape
    outs = [jax.ShapeDtypeStruct((width, 8 * d), BF16)]
    scratch = [pltpu.VMEM((8 * d, width), BF16)]
    return call(join_body, "join", (pos, *pieces), [SM] + [VM] * 4, outs, scratch)[0]


OWN = ((0, 0, 0), (0, 0, 1))
BEHIND = ((0, -1, 0), (0, -1, 1))
AHEAD = ((0, 1, 1), (0, 1, 0))
FAR = ((0, 2, 0), (0, 2, 1))


def mirrored(places):
    return tuple((1 - dy, dx, dc) for dy, dx, dc in places)


def weight_row(pos_ref, place, depth):
    dy, dx, dc = place
    c, x, yh = pos_ref[2], pos_ref[3], pos_ref[4]
    side = lax.rem(x + dx * (1 - 2 * c) + 4, 4)
    block = (lax.rem(yh + dy, 2) * 4 + side) * 2 + lax.rem(c + dc, 2)
    return pl.multiple_of(block * depth, depth)


def view(ref, h):
    return ref[h * 256 : (h + 1) * 256, :]


class Operands:
    def __init__(self):
        self.arrays = []

    def add(self, block):
        array, h = block if isinstance(block, tuple) else (block, 0)
        for i, known in enumerate(self.arrays):
            if known is array:
                return i, h
        self.arrays.append(array)
        return len(self.arrays) - 1, h


def squared(w):
    wide = w.astype(F32)
    return jnp.sum((wide * wide).reshape(w.shape[0] // 8, 8, w.shape[1]), axis=0)


def plus(a, b):
    return b if a is None else a + b


def tiles(cols):
    return [slice(lo, lo + TN) for lo in range(0, cols, TN)]


def nt(a, b):
    return lax.dot_general(a, b, NT, preferred_element_type=F32)


def spread_and_gram(refs, pans, spread, gram):
    for _, (i, g), (k, h) in pans:
        d = view(refs[k], h)
        spread = plus(spread, nt(view(refs[i], g), d))
        gram = plus(gram, nt(d, d))
    return spread, gram


def accumulators(cols, with_base, with_norm):
    shapes = [(256, cols), (8, cols)] * with_base + [(256, cols), (512, 256)] * with_norm
    return [jax.ShapeDtypeStruct(shape, F32) for shape in shapes]


def first_step(pos, both, toks, weight):
    ops = Operands()
    both = [(p, ops.add(t), ops.add(d)) for p, t, d in both]
    toks = [(p, ops.add(t)) for p, t in toks]
    count = len(ops.arrays)
    rows, cols = weight.shape
    depth = ops.arrays[0].shape[1]
    order = [item[0] for item in both + toks]
    order += [p for p in OWN + BEHIND + AHEAD + FAR if p not in order]
    order += mirrored(OWN + BEHIND + AHEAD + FAR)

    def body(pos_ref, *refs):
        hbm = refs[count]
        w_ref, base_out, sq_out, cross_out, both_out, sems = refs[count + 1 :]
        starts, copies = [], []
        for i, p in enumerate(order):
            starts.append(weight_row(pos_ref, p, depth))
            at = pl.ds(starts[i], depth)
            copies.append(pltpu.make_async_copy(hbm.at[at, :], w_ref.at[at, :], sems.at[i]))
            copies[i].start()
        spread, gram = spread_and_gram(refs, both, None, None)
        both_out[:256, :], both_out[256:, :] = spread, gram
        for i, item in enumerate(both + toks):
            copies[i].wait()
            for tile in tiles(cols):
                w = w_ref[pl.ds(starts[i], depth), tile]
                left = jnp.concatenate([view(refs[a], h) for a, h in item[1:]], axis=0)
                part = jnp.dot(left, w, preferred_element_type=F32)
                base, sq = part[:256], squared(w)
                base_out[:, tile] = base if i == 0 else base_out[:, tile] + base
                sq_out[:, tile] = sq if i == 0 else sq_out[:, tile] + sq
                if i < len(both):
                    cross = part[256:]
                    cross_out[:, tile] = cross if i == 0 else cross_out[:, tile] + cross
        for i in range(len(both + toks), len(order)):
            copies[i].wait()

    return call(
        body,
        "first",
        (pos, *ops.arrays, weight),
        [SM] + [VM] * count + [ANY],
        [jax.ShapeDtypeStruct((rows, cols), BF16)] + accumulators(cols, True, True),
        [pltpu.SemaphoreType.DMA((len(order),))],
        limit=30 * MIB,
    )


def step(name, pos, toks, pans, weight, base, norm):
    ops = Operands()
    toks = [(p, ops.add(t)) for p, t in toks]
    pans = [(p, ops.add(t), ops.add(d)) for p, t, d in pans]
    count = len(ops.arrays)
    depth, cols = ops.arrays[0].shape[1], weight.shape[1]
    state = (list(base) if toks else []) + (list(norm) if pans else [])
    n = len(state)

    def body(pos_ref, *refs):
        w_ref = refs[count]
        ins, outs = refs[count + 1 : count + 1 + n], refs[count + 1 + n :]
        if pans:
            spread, gram = spread_and_gram(refs, pans, ins[-1][:256, :], ins[-1][256:, :])
            outs[-1][:256, :], outs[-1][256:, :] = spread, gram
        tok_rows = [weight_row(pos_ref, item[0], depth) for item in toks]
        pan_rows = [weight_row(pos_ref, item[0], depth) for item in pans]
        for tile in tiles(cols):
            if toks:
                total, sq = ins[0][:, tile], ins[1][:, tile]
                for row, (_, (a, h)) in zip(tok_rows, toks):
                    w = w_ref[pl.ds(row, depth), tile]
                    total = total + jnp.dot(view(refs[a], h), w, preferred_element_type=F32)
                    sq = sq + squared(w)
                outs[0][:, tile], outs[1][:, tile] = total, sq
            if pans:
                total = ins[-2][:, tile]
                for row, (_, _, (a, h)) in zip(pan_rows, pans):
                    w = w_ref[pl.ds(row, depth), tile]
                    total = total + jnp.dot(view(refs[a], h), w, preferred_element_type=F32)
                outs[-2][:, tile] = total

    new = call(
        body,
        name,
        (pos, *ops.arrays, weight, *state),
        [SM] + [VM] * (count + 1 + n),
        accumulators(cols, bool(toks), bool(pans)),
        aliases={count + 2 + i: i for i in range(n)},
    )
    return (new[:2] if toks else base), (new[-2:] if pans else norm)


def last_step(pos, both, pans, weight, base, norm, up, mag, ids):
    ops = Operands()
    both, pans = ([(p, ops.add(t), ops.add(d)) for p, t, d in work] for work in (both, pans))
    count = len(ops.arrays)
    depth, cols = ops.arrays[0].shape[1], weight.shape[1]
    adapters, width, tokens = mag.shape[0], up.shape[0], base[0].shape[0]
    rank = width // adapters

    def body(pos_ref, *refs):
        w_ref, base_ref, sq_ref, cross_ref, both_ref, up_ref, mag_ref, id_ref = refs[count : count + 8]
        out_ref, held, sems = refs[count + 8 :]
        spread, gram = spread_and_gram(refs, both + pans, both_ref[:tokens, :], both_ref[tokens:, :])
        both_rows = [weight_row(pos_ref, item[0], depth) for item in both]
        rows = [weight_row(pos_ref, item[0], depth) for item in pans]
        local = id_ref[...] - (pos_ref[0] * 2 + pos_ref[1]) * adapters
        own = jnp.broadcast_to(local, (128, tokens)).T
        lane = lax.broadcasted_iota(jnp.int32, (tokens, width), 1) // rank
        own_wide = jnp.concatenate([own] * (width // 128), axis=1)
        low = jnp.where(lane == own_wide, spread, 0.0).astype(BF16)
        line = lax.broadcasted_iota(jnp.int32, (width, width), 0) // rank
        side = lax.broadcasted_iota(jnp.int32, (width, width), 1) // rank
        gram = jnp.where(line == side, gram, 0.0)
        gram_hi = gram.astype(BF16)
        gram_lo = (gram - gram_hi.astype(F32)).astype(BF16)
        left = jnp.concatenate([low, gram_hi, gram_lo], axis=0)
        own_tile = jnp.concatenate([own] * (TN // 128), axis=1)
        copies = []
        for n, tile in enumerate(tiles(cols)):
            base, sq, cross = base_ref[:, tile], sq_ref[:, tile], cross_ref[:, tile]
            for row, item in zip(both_rows, both):
                w = w_ref[pl.ds(row, depth), tile]
                pair_of = jnp.concatenate([view(refs[a], h) for a, h in item[1:]], axis=0)
                part = jnp.dot(pair_of, w, preferred_element_type=F32)
                base, cross, sq = base + part[:tokens], cross + part[tokens:], sq + squared(w)
            for row, (_, _, (a, h)) in zip(rows, pans):
                w = w_ref[pl.ds(row, depth), tile]
                cross = cross + jnp.dot(view(refs[a], h), w, preferred_element_type=F32)
            up_tile = up_ref[:, tile]
            prod = jnp.dot(left, up_tile, preferred_element_type=F32)
            bent = prod[tokens : tokens + width] + prod[tokens + width :]
            terms = up_tile.astype(F32) * (2.0 * cross + bent)
            weight_sq = jnp.sum(sq, axis=0, keepdims=True)
            scale = None
            for a in range(adapters):
                mine = jnp.sum(terms[a * rank : (a + 1) * rank], axis=0, keepdims=True)
                gain = mag_ref[a : a + 1, tile] / jnp.sqrt(weight_sq + mine + 1e-6)
                wide = jnp.broadcast_to(gain, (tokens, TN))
                scale = wide if scale is None else jnp.where(own_tile == a, wide, scale)
            held[n] = (scale * (base + prod[:tokens])).astype(BF16)
            copies.append(pltpu.make_async_copy(held.at[n], out_ref.at[:, tile], sems.at[n]))
            copies[n].start()
        for copy in copies:
            copy.wait()

    inputs = (pos, *ops.arrays, weight, *base, *norm, up, mag, ids)
    outs = [jax.ShapeDtypeStruct((tokens, cols), BF16)]
    scratch = [pltpu.VMEM((cols // TN, tokens, TN), BF16), pltpu.SemaphoreType.DMA((cols // TN,))]
    return call(body, "last", inputs, [SM] + [VM] * (count + 8), outs, scratch, out_specs=[ANY])[0]


def on_device(tokens, token_adapter, base_weight, panel_down, panel_up, magnitude):
    adapters, rank, cols = panel_up.shape
    row = lax.axis_index("row").astype(jnp.int32)
    ad = lax.axis_index("ad").astype(jnp.int32)
    pos = jnp.stack([ad // 2, ad % 2, row % 2, row // 2 % 4, row // 8])
    up = panel_up.reshape(adapters * rank, cols)

    line = Line()
    line.ran(pos)
    tc = line.send(core, tokens)
    tr = line.send(ring, tokens)
    mine, away = pack(line.after(pos), panel_down)
    line.ran(away)
    line.got(tc)

    got = line.send(ylo, away)
    tr2 = line.send(ring, tc)
    tp = line.send(pair, tokens)
    t = line.send(core, tc)
    line.got(got, tr, t)

    z1 = line.send(lambda a: zshift(a, 1), jnp.stack([mine[1], got[1]]))
    z3 = line.send(lambda a: zshift(a, -1), jnp.stack([mine[3], got[3]]))
    z2 = line.send(lambda a: zshift(a, 2), jnp.stack([mine[2], got[2]]))
    tf = line.send(ring, tr)
    line.got(z1, z3, z2, tr2, tp, tf)
    d = join(line.after(pos), jnp.stack([mine[0], got[0]]), z1, z2, z3)
    line.ran(d)

    dr = line.send(ring, d)
    dc = line.send(core, d)
    tpc = line.send(core, tp)
    trc = line.send(core, cat(tr, tr2))
    line.got(dc, trc, tpc)
    dr2 = line.send(ring, dc)
    dp = line.send(pair, d)
    df = line.send(ring, dr)
    tpr = line.send(ring, cat(tp, tpc))
    w, *sums = first_step(
        line.after(pos),
        list(zip(OWN, [t, tc], [d, dc])),
        list(zip(BEHIND + AHEAD, [tr, tr2, (trc, 0), (trc, 1)])),
        base_weight,
    )
    base, norm = sums[:2], sums[2:]
    line.ran(norm[1])
    line.got(dr2, dp, df, tpr)

    dpc = line.send(core, dp)
    drc = line.send(core, cat(dr, dr2))
    tprc = line.send(core, tpr)
    tfc = line.send(core, tf)
    dfp = line.send(pair, df)
    dpr = line.send(ring, cat(dp, dpc))
    tfp = line.send(ring, tpr[:256])
    dfc = line.send(core, df)
    ring_t = [(tpr, 0), (tpr, 1), (tprc, 0), (tprc, 1)]
    base, norm = step(
        "middle",
        line.after(pos),
        list(zip(FAR + mirrored(OWN + BEHIND + AHEAD), [tf, tfc, tp, tpc] + ring_t)),
        list(
            zip(
                BEHIND + AHEAD + mirrored(OWN),
                [tr, tr2, (trc, 0), (trc, 1), tp, tpc],
                [dr, dr2, (drc, 0), (drc, 1), dp, dpc],
            )
        ),
        w,
        base,
        norm,
    )
    line.ran(norm[1])
    line.got(dfp, dpr, tfp, dfc)

    dprc = line.send(core, dpr)
    dfpc = line.send(core, dfp)
    tfpc = line.send(core, tfp)
    base, norm = step("far", line.after(pos), [], list(zip(FAR, [tf, tfc], [df, dfc])), w, base, norm)
    line.ran(norm[1])
    line.got(dfpc, dprc, tfpc)
    ring_d = [(dpr, 0), (dpr, 1), (dprc, 0), (dprc, 1)]
    return last_step(
        line.after(pos),
        list(zip(mirrored(FAR), [tfp, tfpc], [dfp, dfpc])),
        list(zip(mirrored(BEHIND + AHEAD), ring_t, ring_d)),
        w,
        base,
        norm,
        up,
        magnitude,
        token_adapter[None, :],
    )


def solution(mesh):
    placed = (
        P("ad", "row"),
        P("ad"),
        P(None, "row"),
        P(None, ("row", "ad"), None),
        P("ad", None, "row"),
        P("ad", "row"),
    )
    return jax.shard_map(on_device, mesh=mesh, in_specs=placed, out_specs=P("ad", "row"), check_vma=False)
```

```python
import jax
import jax.numpy as jnp
from jax import lax
from jax.experimental import pallas as pl
from jax.experimental.pallas import tpu as pltpu
from jax.sharding import PartitionSpec as P

F32, BF16 = jnp.float32, jnp.bfloat16
ANY = pl.BlockSpec(memory_space=pltpu.HBM)
VM = pl.BlockSpec(memory_space=pltpu.VMEM)
SM = pl.BlockSpec(memory_space=pltpu.SMEM)
NT = (((1,), (1,)), ((), ()))
TN = 512
MIB = 1 << 20

ROWS = [(yh, x, c) for yh in range(2) for x in range(4) for c in range(2)]
ADS = [(z, yl) for z in range(4) for yl in range(2)]


def row_of(yh, x, c):
    return (yh * 4 + x) * 2 + c


RING = [(row_of(yh, x, c), row_of(yh, (x + 1 - 2 * c) % 4, c)) for yh, x, c in ROWS]
CORE = [(row_of(yh, x, c), row_of(yh, x, 1 - c)) for yh, x, c in ROWS]
PAIR = [(row_of(yh, x, c), row_of(1 - yh, x, c)) for yh, x, c in ROWS]
YLO = [(z * 2 + yl, z * 2 + 1 - yl) for z, yl in ADS]


def ring(a):
    return lax.ppermute(a, "row", RING)


def core(a):
    return lax.ppermute(a, "row", CORE)


def pair(a):
    return lax.ppermute(a, "row", PAIR)


def ylo(a):
    return lax.ppermute(a, "ad", YLO)


def zshift(a, step):
    return lax.ppermute(a, "ad", [(z * 2 + yl, (z + step) % 4 * 2 + yl) for z, yl in ADS])


class Line:
    def __init__(self):
        self.done = ()

    def after(self, a):
        return lax.optimization_barrier((a, *self.done))[0] if self.done else a

    def send(self, how, a):
        return how(self.after(a))

    def got(self, *values):
        self.done += values

    def ran(self, value):
        self.done = (value,)


def cat(*parts):
    return jnp.concatenate(parts, 0)


def cost():
    return pl.CostEstimate(flops=1024, bytes_accessed=1024, transcendentals=0)


def call(body, name, inputs, specs, outs, scratch=(), aliases=None, limit=8 * MIB, out_specs=None):
    return pl.pallas_call(
        body,
        out_shape=outs,
        in_specs=specs,
        out_specs=out_specs or [VM] * len(outs),
        scratch_shapes=list(scratch),
        input_output_aliases=aliases or {},
        name=name,
        cost_estimate=cost(),
        compiler_params=pltpu.CompilerParams(vmem_limit_bytes=limit),
    )(*inputs)


def pack_body(pos_ref, d_ref, mine_ref, send_ref):
    z, yl = pos_ref[0], pos_ref[1]
    for out_ref, lane in ((mine_ref, yl), (send_ref, 1 - yl)):
        for j in range(4):
            group = lax.rem(z + j, 4) * 2 + lane
            four = d_ref[pl.ds(group * 4, 4)]
            out_ref[j] = jnp.concatenate([four[a] for a in range(4)], axis=1)


def pack(pos, panel):
    d, r = panel.shape[1:]
    shape = jax.ShapeDtypeStruct((4, d, 4 * r), BF16)
    return call(pack_body, "pack", (pos, panel), [SM, VM], [shape, shape])


def join_body(pos_ref, a0, a1, a2, a3, out_ref, full):
    z, yl = pos_ref[0], pos_ref[1]
    d = a0.shape[1]
    for ref, back in ((a0, 0), (a1, 3), (a2, 2), (a3, 1)):
        src = lax.rem(z + back, 4) * 2
        full[pl.ds(pl.multiple_of((src + yl) * d, d), d), :] = ref[0]
        full[pl.ds(pl.multiple_of((src + 1 - yl) * d, d), d), :] = ref[1]
    out_ref[...] = full[...].T


def join(pos, *pieces):
    _, d, width = pieces[0].shape
    outs = [jax.ShapeDtypeStruct((width, 8 * d), BF16)]
    scratch = [pltpu.VMEM((8 * d, width), BF16)]
    return call(join_body, "join", (pos, *pieces), [SM] + [VM] * 4, outs, scratch)[0]


OWN = ((0, 0, 0), (0, 0, 1))
BEHIND = ((0, -1, 0), (0, -1, 1))
AHEAD = ((0, 1, 1), (0, 1, 0))
FAR = ((0, 2, 0), (0, 2, 1))


def mirrored(places):
    return tuple((1 - dy, dx, dc) for dy, dx, dc in places)


def weight_row(pos_ref, place, depth):
    dy, dx, dc = place
    c, x, yh = pos_ref[2], pos_ref[3], pos_ref[4]
    side = lax.rem(x + dx * (1 - 2 * c) + 4, 4)
    block = (lax.rem(yh + dy, 2) * 4 + side) * 2 + lax.rem(c + dc, 2)
    return pl.multiple_of(block * depth, depth)


def view(ref, h):
    return ref[h * 256 : (h + 1) * 256, :]


class Operands:
    def __init__(self):
        self.arrays = []

    def add(self, block):
        array, h = block if isinstance(block, tuple) else (block, 0)
        for i, known in enumerate(self.arrays):
            if known is array:
                return i, h
        self.arrays.append(array)
        return len(self.arrays) - 1, h


def squared(w):
    wide = w.astype(F32)
    return jnp.sum((wide * wide).reshape(w.shape[0] // 8, 8, w.shape[1]), axis=0)


def plus(a, b):
    return b if a is None else a + b


def tiles(cols):
    return [slice(lo, lo + TN) for lo in range(0, cols, TN)]


def nt(a, b):
    return lax.dot_general(a, b, NT, preferred_element_type=F32)


def spread_and_gram(refs, pans, spread, gram):
    for _, (i, g), (k, h) in pans:
        d = view(refs[k], h)
        spread = plus(spread, nt(view(refs[i], g), d))
        gram = plus(gram, nt(d, d))
    return spread, gram


def accumulators(cols, with_base, with_norm):
    shapes = [(256, cols), (8, cols)] * with_base + [(256, cols), (512, 256)] * with_norm
    return [jax.ShapeDtypeStruct(shape, F32) for shape in shapes]


def first_step(pos, both, toks, weight):
    ops = Operands()
    both = [(p, ops.add(t), ops.add(d)) for p, t, d in both]
    toks = [(p, ops.add(t)) for p, t in toks]
    count = len(ops.arrays)
    rows, cols = weight.shape
    depth = ops.arrays[0].shape[1]
    order = [item[0] for item in both + toks]
    order += [p for p in OWN + BEHIND + AHEAD + FAR if p not in order]
    order += mirrored(OWN + BEHIND + AHEAD + FAR)

    def body(pos_ref, *refs):
        hbm = refs[count]
        w_ref, base_out, sq_out, cross_out, both_out, sems = refs[count + 1 :]
        starts, copies = [], []
        for i, p in enumerate(order):
            starts.append(weight_row(pos_ref, p, depth))
            at = pl.ds(starts[i], depth)
            copies.append(pltpu.make_async_copy(hbm.at[at, :], w_ref.at[at, :], sems.at[i]))
            copies[i].start()
        spread, gram = spread_and_gram(refs, both, None, None)
        both_out[:256, :], both_out[256:, :] = spread, gram
        for i, item in enumerate(both + toks):
            copies[i].wait()
            for tile in tiles(cols):
                w = w_ref[pl.ds(starts[i], depth), tile]
                left = jnp.concatenate([view(refs[a], h) for a, h in item[1:]], axis=0)
                part = jnp.dot(left, w, preferred_element_type=F32)
                base, sq = part[:256], squared(w)
                base_out[:, tile] = base if i == 0 else base_out[:, tile] + base
                sq_out[:, tile] = sq if i == 0 else sq_out[:, tile] + sq
                if i < len(both):
                    cross = part[256:]
                    cross_out[:, tile] = cross if i == 0 else cross_out[:, tile] + cross
        for i in range(len(both + toks), len(order)):
            copies[i].wait()

    return call(
        body,
        "first",
        (pos, *ops.arrays, weight),
        [SM] + [VM] * count + [ANY],
        [jax.ShapeDtypeStruct((rows, cols), BF16)] + accumulators(cols, True, True),
        [pltpu.SemaphoreType.DMA((len(order),))],
        limit=30 * MIB,
    )


def step(name, pos, toks, pans, weight, base, norm):
    ops = Operands()
    toks = [(p, ops.add(t)) for p, t in toks]
    pans = [(p, ops.add(t), ops.add(d)) for p, t, d in pans]
    count = len(ops.arrays)
    depth, cols = ops.arrays[0].shape[1], weight.shape[1]
    state = (list(base) if toks else []) + (list(norm) if pans else [])
    n = len(state)

    def body(pos_ref, *refs):
        w_ref = refs[count]
        ins, outs = refs[count + 1 : count + 1 + n], refs[count + 1 + n :]
        if pans:
            spread, gram = spread_and_gram(refs, pans, ins[-1][:256, :], ins[-1][256:, :])
            outs[-1][:256, :], outs[-1][256:, :] = spread, gram
        tok_rows = [weight_row(pos_ref, item[0], depth) for item in toks]
        pan_rows = [weight_row(pos_ref, item[0], depth) for item in pans]
        for tile in tiles(cols):
            if toks:
                total, sq = ins[0][:, tile], ins[1][:, tile]
                for row, (_, (a, h)) in zip(tok_rows, toks):
                    w = w_ref[pl.ds(row, depth), tile]
                    total = total + jnp.dot(view(refs[a], h), w, preferred_element_type=F32)
                    sq = sq + squared(w)
                outs[0][:, tile], outs[1][:, tile] = total, sq
            if pans:
                total = ins[-2][:, tile]
                for row, (_, _, (a, h)) in zip(pan_rows, pans):
                    w = w_ref[pl.ds(row, depth), tile]
                    total = total + jnp.dot(view(refs[a], h), w, preferred_element_type=F32)
                outs[-2][:, tile] = total

    new = call(
        body,
        name,
        (pos, *ops.arrays, weight, *state),
        [SM] + [VM] * (count + 1 + n),
        accumulators(cols, bool(toks), bool(pans)),
        aliases={count + 2 + i: i for i in range(n)},
    )
    return (new[:2] if toks else base), (new[-2:] if pans else norm)


def last_step(pos, both, pans, weight, base, norm, up, mag, ids):
    ops = Operands()
    both, pans = ([(p, ops.add(t), ops.add(d)) for p, t, d in work] for work in (both, pans))
    count = len(ops.arrays)
    depth, cols = ops.arrays[0].shape[1], weight.shape[1]
    adapters, width, tokens = mag.shape[0], up.shape[0], base[0].shape[0]
    rank = width // adapters

    def body(pos_ref, *refs):
        w_ref, base_ref, sq_ref, cross_ref, both_ref, up_ref, mag_ref, id_ref = refs[count : count + 8]
        out_ref, held, sems = refs[count + 8 :]
        spread, gram = spread_and_gram(refs, both + pans, both_ref[:tokens, :], both_ref[tokens:, :])
        both_rows = [weight_row(pos_ref, item[0], depth) for item in both]
        rows = [weight_row(pos_ref, item[0], depth) for item in pans]
        local = id_ref[...] - (pos_ref[0] * 2 + pos_ref[1]) * adapters
        own = jnp.broadcast_to(local, (128, tokens)).T
        lane = lax.broadcasted_iota(jnp.int32, (tokens, width), 1) // rank
        own_wide = jnp.concatenate([own] * (width // 128), axis=1)
        low = jnp.where(lane == own_wide, spread, 0.0).astype(BF16)
        line = lax.broadcasted_iota(jnp.int32, (width, width), 0) // rank
        side = lax.broadcasted_iota(jnp.int32, (width, width), 1) // rank
        gram = jnp.where(line == side, gram, 0.0)
        gram_hi = gram.astype(BF16)
        gram_lo = (gram - gram_hi.astype(F32)).astype(BF16)
        left = jnp.concatenate([low, gram_hi, gram_lo], axis=0)
        own_tile = jnp.concatenate([own] * (TN // 128), axis=1)
        copies = []
        for n, tile in enumerate(tiles(cols)):
            base, sq, cross = base_ref[:, tile], sq_ref[:, tile], cross_ref[:, tile]
            for row, item in zip(both_rows, both):
                w = w_ref[pl.ds(row, depth), tile]
                pair_of = jnp.concatenate([view(refs[a], h) for a, h in item[1:]], axis=0)
                part = jnp.dot(pair_of, w, preferred_element_type=F32)
                base, cross, sq = base + part[:tokens], cross + part[tokens:], sq + squared(w)
            for row, (_, _, (a, h)) in zip(rows, pans):
                w = w_ref[pl.ds(row, depth), tile]
                cross = cross + jnp.dot(view(refs[a], h), w, preferred_element_type=F32)
            up_tile = up_ref[:, tile]
            prod = jnp.dot(left, up_tile, preferred_element_type=F32)
            bent = prod[tokens : tokens + width] + prod[tokens + width :]
            terms = up_tile.astype(F32) * (2.0 * cross + bent)
            weight_sq = jnp.sum(sq, axis=0, keepdims=True)
            scale = None
            for a in range(adapters):
                mine = jnp.sum(terms[a * rank : (a + 1) * rank], axis=0, keepdims=True)
                gain = mag_ref[a : a + 1, tile] / jnp.sqrt(weight_sq + mine + 1e-6)
                wide = jnp.broadcast_to(gain, (tokens, TN))
                scale = wide if scale is None else jnp.where(own_tile == a, wide, scale)
            held[n] = (scale * (base + prod[:tokens])).astype(BF16)
            copies.append(pltpu.make_async_copy(held.at[n], out_ref.at[:, tile], sems.at[n]))
            copies[n].start()
        for copy in copies:
            copy.wait()

    inputs = (pos, *ops.arrays, weight, *base, *norm, up, mag, ids)
    outs = [jax.ShapeDtypeStruct((tokens, cols), BF16)]
    scratch = [pltpu.VMEM((cols // TN, tokens, TN), BF16), pltpu.SemaphoreType.DMA((cols // TN,))]
    return call(body, "last", inputs, [SM] + [VM] * (count + 8), outs, scratch, out_specs=[ANY])[0]


def on_device(tokens, token_adapter, base_weight, panel_down, panel_up, magnitude):
    adapters, rank, cols = panel_up.shape
    row = lax.axis_index("row").astype(jnp.int32)
    ad = lax.axis_index("ad").astype(jnp.int32)
    pos = jnp.stack([ad // 2, ad % 2, row % 2, row // 2 % 4, row // 8])
    up = panel_up.reshape(adapters * rank, cols)

    line = Line()
    line.ran(pos)
    tc = line.send(core, tokens)
    tr = line.send(ring, tokens)
    mine, away = pack(line.after(pos), panel_down)
    line.ran(away)
    line.got(tc)

    got = line.send(ylo, away)
    tr2 = line.send(ring, tc)
    tp = line.send(pair, tokens)
    t = line.send(core, tc)
    line.got(got, tr, t)

    z1 = line.send(lambda a: zshift(a, 1), jnp.stack([mine[1], got[1]]))
    z3 = line.send(lambda a: zshift(a, -1), jnp.stack([mine[3], got[3]]))
    z2 = line.send(lambda a: zshift(a, 2), jnp.stack([mine[2], got[2]]))
    tf = line.send(ring, tr)
    line.got(z1, z3, z2, tr2, tp, tf)
    d = join(line.after(pos), jnp.stack([mine[0], got[0]]), z1, z2, z3)
    line.ran(d)

    dr = line.send(ring, d)
    dc = line.send(core, d)
    tpc = line.send(core, tp)
    trc = line.send(core, cat(tr, tr2))
    line.got(dc, trc, tpc)
    dr2 = line.send(ring, dc)
    dp = line.send(pair, d)
    df = line.send(ring, dr)
    tpr = line.send(ring, cat(tp, tpc))
    w, *sums = first_step(
        line.after(pos),
        list(zip(OWN, [t, tc], [d, dc])),
        list(zip(BEHIND + AHEAD, [tr, tr2, (trc, 0), (trc, 1)])),
        base_weight,
    )
    base, norm = sums[:2], sums[2:]
    line.ran(norm[1])
    line.got(dr2, dp, df, tpr)

    dpc = line.send(core, dp)
    drc = line.send(core, cat(dr, dr2))
    tprc = line.send(core, tpr)
    tfc = line.send(core, tf)
    dfp = line.send(pair, df)
    dpr = line.send(ring, cat(dp, dpc))
    tfp = line.send(ring, tpr[:256])
    dfc = line.send(core, df)
    ring_t = [(tpr, 0), (tpr, 1), (tprc, 0), (tprc, 1)]
    base, norm = step(
        "middle",
        line.after(pos),
        list(zip(FAR + mirrored(OWN + BEHIND + AHEAD), [tf, tfc, tp, tpc] + ring_t)),
        list(
            zip(
                BEHIND + AHEAD + mirrored(OWN) + FAR[:1],
                [tr, tr2, (trc, 0), (trc, 1), tp, tpc, tf],
                [dr, dr2, (drc, 0), (drc, 1), dp, dpc, df],
            )
        ),
        w,
        base,
        norm,
    )
    line.ran(norm[1])
    line.got(dfp, dpr, tfp, dfc)

    dprc = line.send(core, dpr)
    dfpc = line.send(core, dfp)
    tfpc = line.send(core, tfp)
    base, norm = step(
        "far",
        line.after(pos),
        [],
        list(zip(FAR[1:] + mirrored(BEHIND), [tfc, *ring_t[:2]], [dfc, (dpr, 0), (dpr, 1)])),
        w,
        base,
        norm,
    )
    line.ran(norm[1])
    line.got(dfpc, dprc, tfpc)
    return last_step(
        line.after(pos),
        list(zip(mirrored(FAR), [tfp, tfpc], [dfp, dfpc])),
        list(zip(mirrored(AHEAD), ring_t[2:], [(dprc, 0), (dprc, 1)])),
        w,
        base,
        norm,
        up,
        magnitude,
        token_adapter[None, :],
    )


def solution(mesh):
    placed = (
        P("ad", "row"),
        P("ad"),
        P(None, "row"),
        P(None, ("row", "ad"), None),
        P("ad", None, "row"),
        P("ad", "row"),
    )
    return jax.shard_map(on_device, mesh=mesh, in_specs=placed, out_specs=P("ad", "row"), check_vma=False)
```

```python
import jax
import jax.numpy as jnp
from jax import lax
from jax.experimental import pallas as pl
from jax.experimental.pallas import tpu as pltpu
from jax.sharding import PartitionSpec as P

F32, BF16 = jnp.float32, jnp.bfloat16
ANY = pl.BlockSpec(memory_space=pltpu.HBM)
VM = pl.BlockSpec(memory_space=pltpu.VMEM)
SM = pl.BlockSpec(memory_space=pltpu.SMEM)
NT = (((1,), (1,)), ((), ()))
TN = 512
MIB = 1 << 20

ROWS = [(yh, x, c) for yh in range(2) for x in range(4) for c in range(2)]
ADS = [(z, yl) for z in range(4) for yl in range(2)]


def row_of(yh, x, c):
    return (yh * 4 + x) * 2 + c


RING = [(row_of(yh, x, c), row_of(yh, (x + 1 - 2 * c) % 4, c)) for yh, x, c in ROWS]
CORE = [(row_of(yh, x, c), row_of(yh, x, 1 - c)) for yh, x, c in ROWS]
PAIR = [(row_of(yh, x, c), row_of(1 - yh, x, c)) for yh, x, c in ROWS]
YLO = [(z * 2 + yl, z * 2 + 1 - yl) for z, yl in ADS]


def ring(a):
    return lax.ppermute(a, "row", RING)


def core(a):
    return lax.ppermute(a, "row", CORE)


def pair(a):
    return lax.ppermute(a, "row", PAIR)


def ylo(a):
    return lax.ppermute(a, "ad", YLO)


def zshift(a, step):
    return lax.ppermute(a, "ad", [(z * 2 + yl, (z + step) % 4 * 2 + yl) for z, yl in ADS])


class Line:
    def __init__(self):
        self.done = ()

    def after(self, a):
        return lax.optimization_barrier((a, *self.done))[0] if self.done else a

    def send(self, how, a):
        return how(self.after(a))

    def got(self, *values):
        self.done += values

    def ran(self, value):
        self.done = (value,)


def cat(*parts):
    return jnp.concatenate(parts, 0)


def cost():
    return pl.CostEstimate(flops=1024, bytes_accessed=1024, transcendentals=0)


def call(body, name, inputs, specs, outs, scratch=(), aliases=None, limit=8 * MIB, out_specs=None):
    return pl.pallas_call(
        body,
        out_shape=outs,
        in_specs=specs,
        out_specs=out_specs or [VM] * len(outs),
        scratch_shapes=list(scratch),
        input_output_aliases=aliases or {},
        name=name,
        cost_estimate=cost(),
        compiler_params=pltpu.CompilerParams(vmem_limit_bytes=limit),
    )(*inputs)


def pack_body(pos_ref, d_ref, mine_ref, send_ref):
    z, yl = pos_ref[0], pos_ref[1]
    for out_ref, lane in ((mine_ref, yl), (send_ref, 1 - yl)):
        for j in range(4):
            group = lax.rem(z + j, 4) * 2 + lane
            four = d_ref[pl.ds(group * 4, 4)]
            out_ref[j] = jnp.concatenate([four[a] for a in range(4)], axis=1)


def pack(pos, panel):
    d, r = panel.shape[1:]
    shape = jax.ShapeDtypeStruct((4, d, 4 * r), BF16)
    return call(pack_body, "pack", (pos, panel), [SM, VM], [shape, shape])


def join_body(pos_ref, a0, a1, a2, a3, out_ref, full):
    z, yl = pos_ref[0], pos_ref[1]
    d = a0.shape[1]
    for ref, back in ((a0, 0), (a1, 3), (a2, 2), (a3, 1)):
        src = lax.rem(z + back, 4) * 2
        full[pl.ds(pl.multiple_of((src + yl) * d, d), d), :] = ref[0]
        full[pl.ds(pl.multiple_of((src + 1 - yl) * d, d), d), :] = ref[1]
    out_ref[...] = full[...].T


def join(pos, *pieces):
    _, d, width = pieces[0].shape
    outs = [jax.ShapeDtypeStruct((width, 8 * d), BF16)]
    scratch = [pltpu.VMEM((8 * d, width), BF16)]
    return call(join_body, "join", (pos, *pieces), [SM] + [VM] * 4, outs, scratch)[0]


OWN = ((0, 0, 0), (0, 0, 1))
BEHIND = ((0, -1, 0), (0, -1, 1))
AHEAD = ((0, 1, 1), (0, 1, 0))
FAR = ((0, 2, 0), (0, 2, 1))


def mirrored(places):
    return tuple((1 - dy, dx, dc) for dy, dx, dc in places)


def weight_row(pos_ref, place, depth):
    dy, dx, dc = place
    c, x, yh = pos_ref[2], pos_ref[3], pos_ref[4]
    side = lax.rem(x + dx * (1 - 2 * c) + 4, 4)
    block = (lax.rem(yh + dy, 2) * 4 + side) * 2 + lax.rem(c + dc, 2)
    return pl.multiple_of(block * depth, depth)


def view(ref, h):
    return ref[h * 256 : (h + 1) * 256, :]


class Operands:
    def __init__(self):
        self.arrays = []

    def add(self, block):
        array, h = block if isinstance(block, tuple) else (block, 0)
        for i, known in enumerate(self.arrays):
            if known is array:
                return i, h
        self.arrays.append(array)
        return len(self.arrays) - 1, h


def squared(w):
    wide = w.astype(F32)
    return jnp.sum((wide * wide).reshape(w.shape[0] // 8, 8, w.shape[1]), axis=0)


def plus(a, b):
    return b if a is None else a + b


def tiles(cols):
    return [slice(lo, lo + TN) for lo in range(0, cols, TN)]


def nt(a, b):
    return lax.dot_general(a, b, NT, preferred_element_type=F32)


def spread_and_gram(refs, pans, spread, gram):
    for _, (i, g), (k, h) in pans:
        d = view(refs[k], h)
        spread = plus(spread, nt(view(refs[i], g), d))
        gram = plus(gram, nt(d, d))
    return spread, gram


def accumulators(cols, with_base, with_norm):
    shapes = [(256, cols), (8, cols)] * with_base + [(256, cols), (512, 256)] * with_norm
    return [jax.ShapeDtypeStruct(shape, F32) for shape in shapes]


def first_step(pos, both, toks, weight):
    ops = Operands()
    both = [(p, ops.add(t), ops.add(d)) for p, t, d in both]
    toks = [(p, ops.add(t)) for p, t in toks]
    count = len(ops.arrays)
    rows, cols = weight.shape
    depth = ops.arrays[0].shape[1]
    order = [item[0] for item in both + toks]
    order += [p for p in OWN + BEHIND + AHEAD + FAR if p not in order]
    order += mirrored(OWN + BEHIND + AHEAD + FAR)

    def body(pos_ref, *refs):
        hbm = refs[count]
        w_ref, base_out, sq_out, cross_out, both_out, sems = refs[count + 1 :]
        starts, copies = [], []
        for i, p in enumerate(order):
            starts.append(weight_row(pos_ref, p, depth))
            at = pl.ds(starts[i], depth)
            copies.append(pltpu.make_async_copy(hbm.at[at, :], w_ref.at[at, :], sems.at[i]))
            copies[i].start()
        spread, gram = spread_and_gram(refs, both, None, None)
        both_out[:256, :], both_out[256:, :] = spread, gram
        for i, item in enumerate(both + toks):
            copies[i].wait()
            for tile in tiles(cols):
                w = w_ref[pl.ds(starts[i], depth), tile]
                left = jnp.concatenate([view(refs[a], h) for a, h in item[1:]], axis=0)
                part = jnp.dot(left, w, preferred_element_type=F32)
                base, sq = part[:256], squared(w)
                base_out[:, tile] = base if i == 0 else base_out[:, tile] + base
                sq_out[:, tile] = sq if i == 0 else sq_out[:, tile] + sq
                if i < len(both):
                    cross = part[256:]
                    cross_out[:, tile] = cross if i == 0 else cross_out[:, tile] + cross
        for i in range(len(both + toks), len(order)):
            copies[i].wait()

    return call(
        body,
        "first",
        (pos, *ops.arrays, weight),
        [SM] + [VM] * count + [ANY],
        [jax.ShapeDtypeStruct((rows, cols), BF16)] + accumulators(cols, True, True),
        [pltpu.SemaphoreType.DMA((len(order),))],
        limit=30 * MIB,
    )


def step(name, pos, toks, pans, weight, base, norm):
    ops = Operands()
    toks = [(p, ops.add(t)) for p, t in toks]
    pans = [(p, ops.add(t), ops.add(d)) for p, t, d in pans]
    count = len(ops.arrays)
    depth, cols = ops.arrays[0].shape[1], weight.shape[1]
    state = (list(base) if toks else []) + (list(norm) if pans else [])
    n = len(state)

    def body(pos_ref, *refs):
        w_ref = refs[count]
        ins, outs = refs[count + 1 : count + 1 + n], refs[count + 1 + n :]
        if pans:
            spread, gram = spread_and_gram(refs, pans, ins[-1][:256, :], ins[-1][256:, :])
            outs[-1][:256, :], outs[-1][256:, :] = spread, gram
        tok_rows = [weight_row(pos_ref, item[0], depth) for item in toks]
        pan_rows = [weight_row(pos_ref, item[0], depth) for item in pans]
        for tile in tiles(cols):
            if toks:
                total, sq = ins[0][:, tile], ins[1][:, tile]
                for row, (_, (a, h)) in zip(tok_rows, toks):
                    w = w_ref[pl.ds(row, depth), tile]
                    total = total + jnp.dot(view(refs[a], h), w, preferred_element_type=F32)
                    sq = sq + squared(w)
                outs[0][:, tile], outs[1][:, tile] = total, sq
            if pans:
                total = ins[-2][:, tile]
                for row, (_, _, (a, h)) in zip(pan_rows, pans):
                    w = w_ref[pl.ds(row, depth), tile]
                    total = total + jnp.dot(view(refs[a], h), w, preferred_element_type=F32)
                outs[-2][:, tile] = total

    new = call(
        body,
        name,
        (pos, *ops.arrays, weight, *state),
        [SM] + [VM] * (count + 1 + n),
        accumulators(cols, bool(toks), bool(pans)),
        aliases={count + 2 + i: i for i in range(n)},
    )
    return (new[:2] if toks else base), (new[-2:] if pans else norm)


def last_step(pos, both, pans, weight, base, norm, up, mag, ids):
    ops = Operands()
    both, pans = ([(p, ops.add(t), ops.add(d)) for p, t, d in work] for work in (both, pans))
    count = len(ops.arrays)
    depth, cols = ops.arrays[0].shape[1], weight.shape[1]
    adapters, width, tokens = mag.shape[0], up.shape[0], base[0].shape[0]
    rank = width // adapters
    parts = [*tiles(cols - TN), *(slice(lo, lo + TN // 2) for lo in range(cols - TN, cols, TN // 2))]

    def body(pos_ref, *refs):
        w_ref, base_ref, sq_ref, cross_ref, both_ref, up_ref, mag_ref, id_ref = refs[count : count + 8]
        out_ref, held, sems = refs[count + 8 :]
        spread, gram = spread_and_gram(refs, both + pans, both_ref[:tokens, :], both_ref[tokens:, :])
        both_rows = [weight_row(pos_ref, item[0], depth) for item in both]
        rows = [weight_row(pos_ref, item[0], depth) for item in pans]
        local = id_ref[...] - (pos_ref[0] * 2 + pos_ref[1]) * adapters
        own = jnp.broadcast_to(local, (128, tokens)).T
        lane = lax.broadcasted_iota(jnp.int32, (tokens, width), 1) // rank
        own_wide = jnp.concatenate([own] * (width // 128), axis=1)
        low = jnp.where(lane == own_wide, spread, 0.0).astype(BF16)
        line = lax.broadcasted_iota(jnp.int32, (width, width), 0) // rank
        side = lax.broadcasted_iota(jnp.int32, (width, width), 1) // rank
        gram = jnp.where(line == side, gram, 0.0)
        gram_hi = gram.astype(BF16)
        gram_lo = (gram - gram_hi.astype(F32)).astype(BF16)
        left = jnp.concatenate([low, gram_hi, gram_lo], axis=0)
        own_wide = jnp.concatenate([own] * (TN // 128), axis=1)
        copies = []
        for n, tile in enumerate(parts):
            span = tile.stop - tile.start
            base, sq, cross = base_ref[:, tile], sq_ref[:, tile], cross_ref[:, tile]
            for row, item in zip(both_rows, both):
                w = w_ref[pl.ds(row, depth), tile]
                pair_of = jnp.concatenate([view(refs[a], h) for a, h in item[1:]], axis=0)
                part = jnp.dot(pair_of, w, preferred_element_type=F32)
                base, cross, sq = base + part[:tokens], cross + part[tokens:], sq + squared(w)
            for row, (_, _, (a, h)) in zip(rows, pans):
                w = w_ref[pl.ds(row, depth), tile]
                cross = cross + jnp.dot(view(refs[a], h), w, preferred_element_type=F32)
            up_tile = up_ref[:, tile]
            prod = jnp.dot(left, up_tile, preferred_element_type=F32)
            bent = prod[tokens : tokens + width] + prod[tokens + width :]
            terms = up_tile.astype(F32) * (2.0 * cross + bent)
            weight_sq = jnp.sum(sq, axis=0, keepdims=True)
            scale = None
            for a in range(adapters):
                mine = jnp.sum(terms[a * rank : (a + 1) * rank], axis=0, keepdims=True)
                gain = mag_ref[a : a + 1, tile] / jnp.sqrt(weight_sq + mine + 1e-6)
                wide = jnp.broadcast_to(gain, (tokens, span))
                scale = wide if scale is None else jnp.where(own_wide[:, :span] == a, wide, scale)
            held[:, tile] = (scale * (base + prod[:tokens])).astype(BF16)
            copies.append(pltpu.make_async_copy(held.at[:, tile], out_ref.at[:, tile], sems.at[n]))
            copies[n].start()
        for copy in copies:
            copy.wait()

    inputs = (pos, *ops.arrays, weight, *base, *norm, up, mag, ids)
    outs = [jax.ShapeDtypeStruct((tokens, cols), BF16)]
    scratch = [pltpu.VMEM((tokens, cols), BF16), pltpu.SemaphoreType.DMA((len(parts),))]
    return call(body, "last", inputs, [SM] + [VM] * (count + 8), outs, scratch, out_specs=[ANY])[0]


def on_device(tokens, token_adapter, base_weight, panel_down, panel_up, magnitude):
    adapters, rank, cols = panel_up.shape
    row = lax.axis_index("row").astype(jnp.int32)
    ad = lax.axis_index("ad").astype(jnp.int32)
    pos = jnp.stack([ad // 2, ad % 2, row % 2, row // 2 % 4, row // 8])
    up = panel_up.reshape(adapters * rank, cols)

    line = Line()
    line.ran(pos)
    tc = line.send(core, tokens)
    tr = line.send(ring, tokens)
    mine, away = pack(line.after(pos), panel_down)
    line.ran(away)
    line.got(tc)

    got = line.send(ylo, away)
    tr2 = line.send(ring, tc)
    tp = line.send(pair, tokens)
    t = line.send(core, tc)
    line.got(got, tr, t)

    z1 = line.send(lambda a: zshift(a, 1), jnp.stack([mine[1], got[1]]))
    z3 = line.send(lambda a: zshift(a, -1), jnp.stack([mine[3], got[3]]))
    z2 = line.send(lambda a: zshift(a, 2), jnp.stack([mine[2], got[2]]))
    tf = line.send(ring, tr)
    line.got(z1, z3, z2, tr2, tp, tf)
    d = join(line.after(pos), jnp.stack([mine[0], got[0]]), z1, z2, z3)
    line.ran(d)

    dr = line.send(ring, d)
    dc = line.send(core, d)
    tpc = line.send(core, tp)
    trc = line.send(core, cat(tr, tr2))
    line.got(dc, trc, tpc)
    dr2 = line.send(ring, dc)
    dp = line.send(pair, d)
    df = line.send(ring, dr)
    tpr = line.send(ring, cat(tp, tpc))
    w, *sums = first_step(
        line.after(pos),
        list(zip(OWN, [t, tc], [d, dc])),
        list(zip(BEHIND + AHEAD, [tr, tr2, (trc, 0), (trc, 1)])),
        base_weight,
    )
    base, norm = sums[:2], sums[2:]
    line.ran(norm[1])
    line.got(dr2, dp, df, tpr)

    dpc = line.send(core, dp)
    drc = line.send(core, cat(dr, dr2))
    tprc = line.send(core, tpr)
    tfc = line.send(core, tf)
    dfp = line.send(pair, df)
    dpr = line.send(ring, cat(dp, dpc))
    tfp = line.send(ring, tpr[:256])
    dfc = line.send(core, df)
    ring_t = [(tpr, 0), (tpr, 1), (tprc, 0), (tprc, 1)]
    base, norm = step(
        "middle",
        line.after(pos),
        list(zip(FAR + mirrored(OWN + BEHIND + AHEAD), [tf, tfc, tp, tpc] + ring_t)),
        list(
            zip(
                BEHIND + AHEAD + mirrored(OWN) + FAR[:1],
                [tr, tr2, (trc, 0), (trc, 1), tp, tpc, tf],
                [dr, dr2, (drc, 0), (drc, 1), dp, dpc, df],
            )
        ),
        w,
        base,
        norm,
    )
    line.ran(norm[1])
    line.got(dfp, dpr, tfp, dfc)

    dprc = line.send(core, dpr)
    dfpc = line.send(core, dfp)
    tfpc = line.send(core, tfp)
    base, norm = step(
        "far",
        line.after(pos),
        [],
        list(zip(FAR[1:] + mirrored(BEHIND), [tfc, *ring_t[:2]], [dfc, (dpr, 0), (dpr, 1)])),
        w,
        base,
        norm,
    )
    line.ran(norm[1])
    line.got(dfpc, dprc, tfpc)
    return last_step(
        line.after(pos),
        list(zip(mirrored(FAR), [tfp, tfpc], [dfp, dfpc])),
        list(zip(mirrored(AHEAD), ring_t[2:], [(dprc, 0), (dprc, 1)])),
        w,
        base,
        norm,
        up,
        magnitude,
        token_adapter[None, :],
    )


def solution(mesh):
    placed = (
        P("ad", "row"),
        P("ad"),
        P(None, "row"),
        P(None, ("row", "ad"), None),
        P("ad", None, "row"),
        P("ad", "row"),
    )
    return jax.shard_map(on_device, mesh=mesh, in_specs=placed, out_specs=P("ad", "row"), check_vma=False)
```
